32 devices in a mesh: groups: 2 (over y), cluster: 4 (over x, core), expert: 4 (over z).
Axes of the slice: x: 2, y: 2, z: 4, core: 2. Of those that a mesh axis runs over, the one named last changes fastest.
Arguments:
- tokens: bfloat16 [2048, 2048], P(('groups', 'cluster', 'expert')), parts along dimension 0, may hold values from -6 to 6
- cluster_ids: int32 [2048], P(('groups', 'cluster', 'expert')), parts along dimension 0, may hold values from 0 to 3, as said below
- expert_ids: int32 [2048, 2], P(('groups', 'cluster', 'expert')), parts along dimension 0, may hold values from 0 to 1, as said below
- gate_probs: bfloat16 [2048, 2], P(('groups', 'cluster', 'expert')), parts along dimension 0, may hold values from 0.19921875 to 1
- w_gate: bfloat16 [16, 2048, 384], P(('cluster', 'expert')), may hold values from -0.125 to 0.125
- w_up: bfloat16 [16, 2048, 384], P(('cluster', 'expert')), may hold values from -0.125 to 0.125
- w_down: bfloat16 [16, 384, 2048], P(('cluster', 'expert')), may hold values from -0.21875 to 0.21875
Outputs:
- mixed: bfloat16 [2048, 2048], P(('groups', 'cluster', 'expert')), parts along dimension 0
The draws below stay inside these ranges and needn't reach their ends.
There are 2 independent parts, one for each index of `groups`. The reference program is written for one: setup_inputs(seed, part) draws one part's arguments, and reference() takes and returns one part's arrays. A program takes and returns all parts, laid end to end along the dimension named above; an argument that names none is the same for every part. Nothing has to cross between parts.
Inputs may be any that keep to these rules, and one draw needn't show every extreme that they name: `cluster_ids`: among the tokens of one device (an aligned block of 64 tokens) at most 32 name the same cluster; in every draw some device has exactly 32 tokens of one cluster. `expert_ids`: A token's two expert numbers differ. Among the tokens of one device at most 32 name the same expert number of the same cluster; in every draw some device reaches 32.
All inputs are finite; a program needn't handle non-finite values.
Results may differ from the reference program's by a relative error of at most 0.0059.
Values may be sent and summed in bfloat16 or wider, within the bound.
A program may use at most 64 MiB of HBM per device.

```python
import jax
import jax.numpy as jnp
from jax import lax

D = 2048
FF = 768
TOK_DEV = 64
CLUSTERS = 4
EPC = 2
EXPERTS = 8
FF_HALF = 384
C1 = 32
C2 = 32
TOKENS = 1024
HALVES = 16


def routing_table(key):
    block_count = TOKENS // TOK_DEV

    def one_block(block_key):
        k_hot, k_slots, k_order, k_perm, k_shift = jax.random.split(block_key, 5)
        hot = jax.random.randint(k_hot, (), 0, CLUSTERS)
        others = (hot + 1 + jnp.arange(CLUSTERS - 1)) % CLUSTERS
        chosen = jax.random.permutation(k_slots, (CLUSTERS - 1) * C1)[:TOK_DEV - C1]
        clusters = jnp.concatenate([jnp.full((C1,), hot, jnp.int32), others[chosen // C1].astype(jnp.int32)])
        clusters = clusters[jax.random.permutation(k_order, TOK_DEV)]
        position = jnp.arange(TOK_DEV)
        earlier = (clusters[:, None] == clusters[None, :]) & (position[None, :] < position[:, None])
        rank = jnp.sum(earlier.astype(jnp.int32), axis=1)
        orders = jax.vmap(lambda sub_key: jax.random.permutation(sub_key, EPC))(jax.random.split(k_perm, CLUSTERS))
        shifts = jax.random.randint(k_shift, (CLUSTERS, C1 // EPC), 1, EPC)
        column = rank % EPC
        first = orders[clusters, column]
        second = orders[clusters, (column + shifts[clusters, rank // EPC]) % EPC]
        return (clusters, jnp.stack([first, second], axis=1))
    clusters, experts = jax.vmap(one_block)(jax.random.split(key, block_count))
    return (clusters.reshape(TOKENS).astype(jnp.int32), experts.reshape(TOKENS, 2).astype(jnp.int32))


def draw_cluster_ids(key, part):
    return routing_table(key)[0]


def draw_expert_ids(key, part):
    return routing_table(key)[1]


def level_of(key, dims, cuts, least, largest):
    def one(axis_at, blocks):
        draws = jax.random.uniform(jax.random.fold_in(jax.random.fold_in(key, 6), axis_at), (blocks,), jnp.float32, least / len(cuts), largest / len(cuts))
        return jnp.repeat(jnp.exp(draws), dims[axis_at] // blocks).reshape((-1,) + (1,) * (len(dims) - axis_at - 1))

    loudness = one(*cuts[0])
    for cut in cuts[1:]:
        loudness = loudness * one(*cut)
    return loudness


def bell_draw(rng, shape, scale, reach, pieces=(), held_as=jnp.bfloat16):
    result = scale * jax.random.normal(rng, shape, jnp.float32)
    if pieces:
        result = result * level_of(rng, shape, pieces, -0.22, 0.18)
    return jnp.clip(result, -reach, reach).astype(held_as)


def setup_inputs(seed: int = 0, part: int = 0) -> dict:
    keys = jax.random.split(jax.random.key(seed), 8)
    part_keys = jax.random.split(jax.random.fold_in(keys[7], part), 8)
    return {
        "tokens": bell_draw(part_keys[0], (TOKENS, D), 1.0, 6.0, ((0, 16),)),
        "cluster_ids": draw_cluster_ids(jax.random.fold_in(jax.random.fold_in(keys[7], part), 71), part),
        "expert_ids": draw_expert_ids(jax.random.fold_in(jax.random.fold_in(keys[7], part), 71), part),
        "gate_probs": jnp.clip(0.19921875 + 0.80078125 * jax.random.uniform(part_keys[3], (TOKENS, 2), jnp.float32) ** level_of(part_keys[3], (TOKENS, 2), ((0, 16),), -0.2, 0.2), 0.19921875, 1.0).astype(jnp.bfloat16),
        "w_gate": bell_draw(keys[4], (HALVES, D, FF_HALF), D ** -0.5, 0.125, ((0, 16),)),
        "w_up": bell_draw(keys[5], (HALVES, D, FF_HALF), D ** -0.5, 0.125, ((0, 16),)),
        "w_down": bell_draw(keys[6], (HALVES, FF_HALF, D), FF ** -0.5, 0.21875, ((0, 16),)),
    }


def apply_expert(rows, gate_mat, up_mat, down_mat):
    gate = jnp.dot(rows, gate_mat, preferred_element_type=jnp.float32)
    up_part = jnp.dot(rows, up_mat, preferred_element_type=jnp.float32)
    hidden = (jax.nn.silu(gate) * up_part).astype(jnp.bfloat16)
    return jnp.dot(hidden, down_mat, preferred_element_type=jnp.float32).astype(jnp.bfloat16)


def reference(tokens, cluster_ids, expert_ids, gate_probs, w_gate, w_up, w_down):
    global_ids = (cluster_ids[:, None] * EPC + expert_ids).reshape(-1).astype(jnp.int32)
    weights_flat = gate_probs.reshape(-1).astype(jnp.float32)
    capacity = C2 * (TOKENS // TOK_DEV)
    slot_index = jnp.arange(capacity, dtype=jnp.int32)

    def visit(total, expert):
        hits = global_ids == expert
        picked = jnp.nonzero(hits, size=capacity, fill_value=0)[0].astype(jnp.int32)
        live = slot_index < jnp.sum(hits.astype(jnp.int32))
        rows = tokens[picked // 2]
        gate_mat = jnp.concatenate([w_gate[2 * expert], w_gate[2 * expert + 1]], axis=1)
        up_mat = jnp.concatenate([w_up[2 * expert], w_up[2 * expert + 1]], axis=1)
        down_mat = jnp.concatenate([w_down[2 * expert], w_down[2 * expert + 1]], axis=0)
        outputs = apply_expert(rows, gate_mat, up_mat, down_mat)
        factor = jnp.where(live, weights_flat[picked], jnp.zeros_like(weights_flat[picked]))
        total = total.at[picked // 2].add(outputs.astype(jnp.float32) * factor[:, None])
        return total, None

    start = jnp.zeros((TOKENS, D), jnp.float32)
    total, unused = lax.scan(visit, start, jnp.arange(EXPERTS, dtype=jnp.int32))
    return total.astype(jnp.bfloat16)
```

```python
import jax
import jax.numpy as jnp
from jax import lax
from jax.sharding import PartitionSpec as P


def routed(tokens, cluster_ids, expert_ids, gate_probs, w_gate, w_up, w_down):
    clusters = lax.axis_size("cluster")
    expert_devs = lax.axis_size("expert")
    per_cluster = expert_devs // 2
    tok_count, feat_dim = tokens.shape
    cap_first = 2 * tok_count // clusters
    cap_second = 2 * cap_first // per_cluster
    stride = clusters * cap_second
    own_cluster = lax.axis_index("cluster")
    pair_key = (cluster_ids[:, None] * per_cluster + expert_ids).reshape(-1)
    pair_pos = jnp.arange(2 * tok_count)
    pair_earlier = (pair_key[:, None] == pair_key[None, :]) & (
        pair_pos[None, :] < pair_pos[:, None]
    )
    pair_slot = jnp.sum(pair_earlier.astype(jnp.int32), axis=1).reshape(tok_count, 2)
    tok_pos = jnp.arange(tok_count)
    tok_earlier = (cluster_ids[:, None] == cluster_ids[None, :]) & (
        tok_pos[None, :] < tok_pos[:, None]
    )
    tok_rank = jnp.sum(tok_earlier.astype(jnp.int32), axis=1)
    first_slot = cluster_ids * cap_first + tok_rank
    target = expert_ids * stride + own_cluster * cap_second + pair_slot
    out_rows = jnp.zeros((clusters * cap_first, feat_dim), jnp.bfloat16).at[first_slot].set(tokens)
    out_target = (
        jnp.full((clusters * cap_first, 2), per_cluster * stride, jnp.int32)
        .at[first_slot]
        .set(target)
    )
    out_gates = jnp.zeros((clusters * cap_first, 2), jnp.bfloat16).at[first_slot].set(gate_probs)
    rows_in, target_in, gates_in = (
        lax.all_to_all(
            out_rows.reshape(clusters, cap_first, feat_dim),
            "cluster",
            split_axis=0,
            concat_axis=0,
            tiled=True,
        ),
        lax.all_to_all(
            out_target.reshape(clusters, cap_first, 2),
            "cluster",
            split_axis=0,
            concat_axis=0,
            tiled=True,
        ),
        lax.all_to_all(
            out_gates.reshape(clusters, cap_first, 2),
            "cluster",
            split_axis=0,
            concat_axis=0,
            tiled=True,
        ),
    )
    flat_rows = rows_in.reshape(-1, feat_dim)
    flat_target = target_in.reshape(-1, 2)
    flat_gates = gates_in.reshape(-1, 2).astype(jnp.float32)
    sectioned = jnp.zeros((per_cluster * stride, feat_dim), jnp.bfloat16)
    sectioned = sectioned.at[flat_target[:, 0]].set(flat_rows, mode="drop")
    sectioned = sectioned.at[flat_target[:, 1]].set(flat_rows, mode="drop")
    sectioned = sectioned.reshape(per_cluster, clusters, cap_second, feat_dim)
    gate_half = w_gate[0]
    up_half = w_up[0]
    down_half = w_down[0]
    send = jnp.repeat(sectioned, 2, axis=0)
    block = lax.all_to_all(send, "expert", split_axis=0, concat_axis=2, tiled=True)
    items = block.shape[1]
    rows = block.reshape(-1, feat_dim)
    gate = jnp.dot(rows, gate_half, preferred_element_type=jnp.float32)
    up_part = jnp.dot(rows, up_half, preferred_element_type=jnp.float32)
    hidden = (jax.nn.silu(gate) * up_part).astype(jnp.bfloat16)
    partial_value = jnp.dot(hidden, down_half, preferred_element_type=jnp.float32).reshape(
        1, items, expert_devs * cap_second, feat_dim
    )
    back = lax.all_to_all(partial_value, "expert", split_axis=2, concat_axis=0, tiled=True)
    summed = jnp.sum(back.reshape(per_cluster, 2, items, cap_second, feat_dim), axis=1)
    expert_out = summed.astype(jnp.bfloat16)
    flat_out = expert_out.reshape(-1, feat_dim)
    safe_target = jnp.minimum(flat_target, per_cluster * stride - 1)
    picked = flat_out[safe_target]
    combined = (
        picked[:, 0].astype(jnp.float32) * flat_gates[:, 0:1]
        + picked[:, 1].astype(jnp.float32) * flat_gates[:, 1:2]
    )
    combined = combined.astype(jnp.bfloat16).reshape(clusters, cap_first, feat_dim)
    back_rows = lax.all_to_all(combined, "cluster", split_axis=0, concat_axis=0, tiled=True)
    return back_rows.reshape(-1, feat_dim)[first_slot]


def dense(tokens, cluster_ids, expert_ids, gate_probs, w_gate, w_up, w_down):
    axes = ("cluster", "expert")
    own_expert = lax.axis_index("cluster") * 2 + lax.axis_index("expert") // 2
    rows = lax.all_gather(tokens, axes, axis=0, tiled=True)
    wanted = jnp.arange(8) == cluster_ids[:, None, None] * 2 + expert_ids[:, :, None]
    table = jnp.sum(jnp.where(wanted, gate_probs.astype(jnp.float32)[:, :, None], 0.0), axis=1)
    table = lax.all_gather(table.T, axes, axis=1, tiled=True)
    weight = lax.dynamic_index_in_dim(table, own_expert, 0, keepdims=False)
    gate = jnp.dot(rows, w_gate[0], preferred_element_type=jnp.float32)
    up_part = jnp.dot(rows, w_up[0], preferred_element_type=jnp.float32)
    hidden = (jax.nn.silu(gate) * up_part).astype(jnp.bfloat16)
    partial = jnp.dot(hidden, w_down[0], preferred_element_type=jnp.float32)
    partial = (partial * weight[:, None]).astype(jnp.bfloat16)
    return lax.psum_scatter(partial, axes, scatter_dimension=0, tiled=True)


def solution(mesh):
    shards = dense if mesh.shape["expert"] == 4 else routed
    in_specs = (
        P(("groups", "cluster", "expert"), None),
        P(("groups", "cluster", "expert")),
        P(("groups", "cluster", "expert"), None),
        P(("groups", "cluster", "expert"), None),
        P(("cluster", "expert"), None, None),
        P(("cluster", "expert"), None, None),
        P(("cluster", "expert"), None, None),
    )
    out_specs = P(("groups", "cluster", "expert"), None)
    return jax.shard_map(shards, mesh=mesh, in_specs=in_specs, out_specs=out_specs, check_vma=False)
```

```python
import jax
import jax.numpy as jnp
from jax import lax
from jax.experimental import pallas as pl
from jax.experimental.pallas import tpu as pltpu
from jax.sharding import PartitionSpec as P


def routed(tokens, cluster_ids, expert_ids, gate_probs, w_gate, w_up, w_down):
    clusters = lax.axis_size("cluster")
    expert_devs = lax.axis_size("expert")
    per_cluster = expert_devs // 2
    tok_count, feat_dim = tokens.shape
    cap_first = 2 * tok_count // clusters
    cap_second = 2 * cap_first // per_cluster
    stride = clusters * cap_second
    own_cluster = lax.axis_index("cluster")
    pair_key = (cluster_ids[:, None] * per_cluster + expert_ids).reshape(-1)
    pair_pos = jnp.arange(2 * tok_count)
    pair_earlier = (pair_key[:, None] == pair_key[None, :]) & (
        pair_pos[None, :] < pair_pos[:, None]
    )
    pair_slot = jnp.sum(pair_earlier.astype(jnp.int32), axis=1).reshape(tok_count, 2)
    tok_pos = jnp.arange(tok_count)
    tok_earlier = (cluster_ids[:, None] == cluster_ids[None, :]) & (
        tok_pos[None, :] < tok_pos[:, None]
    )
    tok_rank = jnp.sum(tok_earlier.astype(jnp.int32), axis=1)
    first_slot = cluster_ids * cap_first + tok_rank
    target = expert_ids * stride + own_cluster * cap_second + pair_slot
    out_rows = jnp.zeros((clusters * cap_first, feat_dim), jnp.bfloat16).at[first_slot].set(tokens)
    out_target = (
        jnp.full((clusters * cap_first, 2), per_cluster * stride, jnp.int32)
        .at[first_slot]
        .set(target)
    )
    out_gates = jnp.zeros((clusters * cap_first, 2), jnp.bfloat16).at[first_slot].set(gate_probs)
    rows_in, target_in, gates_in = (
        lax.all_to_all(
            out_rows.reshape(clusters, cap_first, feat_dim),
            "cluster",
            split_axis=0,
            concat_axis=0,
            tiled=True,
        ),
        lax.all_to_all(
            out_target.reshape(clusters, cap_first, 2),
            "cluster",
            split_axis=0,
            concat_axis=0,
            tiled=True,
        ),
        lax.all_to_all(
            out_gates.reshape(clusters, cap_first, 2),
            "cluster",
            split_axis=0,
            concat_axis=0,
            tiled=True,
        ),
    )
    flat_rows = rows_in.reshape(-1, feat_dim)
    flat_target = target_in.reshape(-1, 2)
    flat_gates = gates_in.reshape(-1, 2).astype(jnp.float32)
    sectioned = jnp.zeros((per_cluster * stride, feat_dim), jnp.bfloat16)
    sectioned = sectioned.at[flat_target[:, 0]].set(flat_rows, mode="drop")
    sectioned = sectioned.at[flat_target[:, 1]].set(flat_rows, mode="drop")
    sectioned = sectioned.reshape(per_cluster, clusters, cap_second, feat_dim)
    gate_half = w_gate[0]
    up_half = w_up[0]
    down_half = w_down[0]
    send = jnp.repeat(sectioned, 2, axis=0)
    block = lax.all_to_all(send, "expert", split_axis=0, concat_axis=2, tiled=True)
    items = block.shape[1]
    rows = block.reshape(-1, feat_dim)
    gate = jnp.dot(rows, gate_half, preferred_element_type=jnp.float32)
    up_part = jnp.dot(rows, up_half, preferred_element_type=jnp.float32)
    hidden = (jax.nn.silu(gate) * up_part).astype(jnp.bfloat16)
    partial_value = jnp.dot(hidden, down_half, preferred_element_type=jnp.float32).reshape(
        1, items, expert_devs * cap_second, feat_dim
    )
    back = lax.all_to_all(partial_value, "expert", split_axis=2, concat_axis=0, tiled=True)
    summed = jnp.sum(back.reshape(per_cluster, 2, items, cap_second, feat_dim), axis=1)
    expert_out = summed.astype(jnp.bfloat16)
    flat_out = expert_out.reshape(-1, feat_dim)
    safe_target = jnp.minimum(flat_target, per_cluster * stride - 1)
    picked = flat_out[safe_target]
    combined = (
        picked[:, 0].astype(jnp.float32) * flat_gates[:, 0:1]
        + picked[:, 1].astype(jnp.float32) * flat_gates[:, 1:2]
    )
    combined = combined.astype(jnp.bfloat16).reshape(clusters, cap_first, feat_dim)
    back_rows = lax.all_to_all(combined, "cluster", split_axis=0, concat_axis=0, tiled=True)
    return back_rows.reshape(-1, feat_dim)[first_slot]


MESH = pl.DeviceIdType.MESH
LANES = 128


def layer_kernel(
    tok_ref, table_ref, wg_hbm, wu_hbm, wd_hbm, out_ref,
    rows, part, core_in, x_in, z_in, wg, wu, wd,
    w_sem, zs, zr, xs, xr, ss, sr, ps, pr, bs, br, cs, cr,
):
    group = lax.axis_index("groups")
    c = lax.axis_index("cluster")
    z = lax.axis_index("expert")
    count, feat = tok_ref.shape
    depth = 4
    twin = (group, c + 1 - 2 * (c % 2), z)
    across = (group, (c + 2) % 4, z)
    below, above = (group, c, z - 1), (group, c, z + 1)
    own_expert = c * 2 + z // 2

    loads = [
        pltpu.make_async_copy(src.at[0], dst, w_sem.at[i])
        for i, (src, dst) in enumerate(((wg_hbm, wg), (wu_hbm, wu), (wd_hbm, wd)))
    ]
    for load in loads:
        load.start()
    rows[z, pl.ds(0, count), pl.ds(0, feat)] = tok_ref[...]
    rows[z, pl.ds(0, count), pl.ds(feat, LANES)] = table_ref[...]

    barrier = pltpu.get_barrier_semaphore()
    pl.semaphore_signal(barrier, inc=1, device_id=twin, device_id_type=MESH)
    pl.semaphore_signal(barrier, inc=1, device_id=across, device_id_type=MESH)

    @pl.when(z > 0)
    def _():
        pl.semaphore_signal(barrier, inc=1, device_id=below, device_id_type=MESH)

    @pl.when(z < depth - 1)
    def _():
        pl.semaphore_signal(barrier, inc=1, device_id=above, device_id_type=MESH)

    middle = (z > 0) & (z < depth - 1)
    pl.semaphore_wait(barrier, 3 + middle.astype(jnp.int32))

    def remote(src, dst, send, recv, device):
        return pltpu.make_async_remote_copy(
            src_ref=src, dst_ref=dst, send_sem=send, recv_sem=recv,
            device_id=device, device_id_type=MESH,
        )

    def block(b, r):
        return rows.at[b, pl.ds(r * count, count)]

    def piece(b, r):
        return part.at[b, pl.ds(r * count, count)]

    def to_z(b, up):
        return remote(block(b, 0), block(b, 0), zs.at[up, b], zr.at[b], above if up else below)

    def to_x(b):
        return remote(block(b, 0), block(b, 2), xs.at[b], xr.at[b], across)

    def to_twin(b, r):
        i = r // 2
        return remote(block(b, r), block(b, r + 1), ss.at[i, b], sr.at[i, b], twin)

    def part_to_twin(b, r):
        i = r // 2
        return remote(piece(b, r), core_in.at[i, b], ps.at[i, b], pr.at[i, b], twin)

    def part_to_x(b):
        return remote(piece(b, 2), x_in.at[b], bs.at[b], br.at[b], across)

    def sum_up(b):
        return remote(piece(b, 0), z_in.at[b], cs.at[b], cr.at[b], above)

    def sum_down(b):
        last = (b == z - 1).astype(jnp.int32)
        slot = b * (1 - last) + depth * last
        return remote(piece(b, 0), z_in.at[slot], cs.at[b], cr.at[slot], below)

    def order(k):
        far = 3 * (2 - z)
        inner = jnp.where(k == 0, z, jnp.where(k == 1, z - 1, jnp.where(k == 2, z + 1, far)))
        return jnp.where(z == 0, k, jnp.where(z == depth - 1, depth - 1 - k, inner))

    def spread(b):
        to_x(b).start()
        to_twin(b, 0).start()

    @pl.when(z < depth - 1)
    def _():
        to_z(z, 1).start()

    @pl.when(z > 0)
    def _():
        to_z(z, 0).start()

    spread(z)

    def fold_core(b):
        part_to_twin(b, 3).wait_recv()
        piece(b, 2)[...] = piece(b, 2)[...] + core_in[1, b]
        part_to_x(b).start()

    def compute(b):
        lhs = rows[b, :, pl.ds(0, feat)]
        gate = jnp.dot(lhs, wg[...], preferred_element_type=jnp.float32)
        up_part = jnp.dot(lhs, wu[...], preferred_element_type=jnp.float32)
        hidden = (gate / (1.0 + jnp.exp(-gate)) * up_part).astype(jnp.bfloat16)
        weights = rows[b, :, pl.ds(feat, LANES)].astype(jnp.float32)
        lane = lax.broadcasted_iota(jnp.int32, weights.shape, 1)
        weight = jnp.sum(jnp.where(lane == own_expert, weights, 0.0), axis=1, keepdims=True)
        tile = min(feat, 512)
        for n in range(feat // tile):
            cols = pl.ds(n * tile, tile)
            out = jnp.dot(hidden, wd[:, cols], preferred_element_type=jnp.float32)
            part[b, :, cols] = (out * weight).astype(jnp.bfloat16)

    def stage(d, carry):
        for side in (-1, 1):
            b = z + side * d

            @pl.when((d < depth) & (b >= 0) & (b < depth))
            def _():
                to_z(b, 0).wait_recv()
                if side < 0:

                    @pl.when(z < depth - 1)
                    def _():
                        to_z(b, 1).start()
                else:

                    @pl.when(z > 0)
                    def _():
                        to_z(b, 0).start()

                spread(b)

        b = order(d - 1)
        to_x(b).wait_recv()
        to_twin(b, 2).start()

        @pl.when(d == depth)
        def _():
            fold_core(order(depth - 2))

        @pl.when(d == 1)
        def _():
            for load in loads:
                load.wait()

        to_twin(b, 0).wait_recv()
        to_twin(b, 2).wait_recv()
        compute(b)
        part_to_twin(b, 3).start()
        part_to_twin(b, 1).start()
        return carry

    lax.fori_loop(1, depth + 1, stage, 0)
    for k in (3, 1, 0):
        fold_core(order(k))

    def total(b):
        part_to_twin(b, 1).wait_recv()
        part_to_x(b).wait_recv()
        value = piece(b, 0)[...].astype(jnp.float32) + core_in[0, b].astype(jnp.float32)
        return value + x_in[b].astype(jnp.float32)

    def fold(j, carry):
        b = order(jnp.where(j == 0, 2, jnp.where(j == 1, 3, 1)))
        piece(b, 0)[...] = total(b).astype(jnp.bfloat16)

        @pl.when(((b > z) & (z > 0)) | ((b < z) & (z < depth - 1)))
        def _():
            sum_up(b).wait_recv()
            mine = piece(b, 0)[...].astype(jnp.float32)
            piece(b, 0)[...] = (mine + z_in[b].astype(jnp.float32)).astype(jnp.bfloat16)

        @pl.when(b > z)
        def _():
            sum_up(b).start()

        @pl.when(b < z)
        def _():
            sum_down(b).start()

        return carry

    lax.fori_loop(0, depth - 1, fold, 0)
    out_ref[...] = total(z).astype(jnp.bfloat16)
    for slot, there in ((z, z > 0), (depth, z < depth - 1)):

        @pl.when(there)
        def _():
            remote(piece(z, 0), z_in.at[slot], cs.at[z], cr.at[slot], across).wait_recv()
            mine = out_ref[...].astype(jnp.float32)
            out_ref[...] = (mine + z_in[slot].astype(jnp.float32)).astype(jnp.bfloat16)

    def drain(b, carry):
        @pl.when((z < depth - 1) & (b <= z))
        def _():
            to_z(b, 1).wait_send()

        @pl.when((z > 0) & (b >= z))
        def _():
            to_z(b, 0).wait_send()

        to_x(b).wait_send()
        to_twin(b, 0).wait_send()
        to_twin(b, 2).wait_send()
        part_to_twin(b, 1).wait_send()
        part_to_twin(b, 3).wait_send()
        part_to_x(b).wait_send()

        @pl.when(b != z)
        def _():
            sum_up(b).wait_send()

        return carry

    lax.fori_loop(0, depth, drain, 0)


def fused(tokens, cluster_ids, expert_ids, gate_probs, w_gate, w_up, w_down):
    count, feat = tokens.shape
    half = w_gate.shape[2]
    lane = jnp.arange(LANES)
    pair = cluster_ids[:, None] * 2 + expert_ids
    table = jnp.where(pair[:, 0:1] == lane, gate_probs[:, 0:1], 0)
    table = jnp.where(pair[:, 1:2] == lane, gate_probs[:, 1:2], table).astype(jnp.bfloat16)
    vmem = pl.BlockSpec(memory_space=pltpu.VMEM)
    hbm = pl.BlockSpec(memory_space=pl.ANY)
    b16 = jnp.bfloat16
    dma = pltpu.SemaphoreType.DMA
    return pl.pallas_call(
        layer_kernel,
        out_shape=jax.ShapeDtypeStruct((count, feat), b16),
        in_specs=[vmem, vmem, hbm, hbm, hbm],
        out_specs=vmem,
        scratch_shapes=[
            pltpu.VMEM((4, 4 * count, feat + LANES), b16),
            pltpu.VMEM((4, 4 * count, feat), b16),
            pltpu.VMEM((2, 4, count, feat), b16),
            pltpu.VMEM((4, count, feat), b16),
            pltpu.VMEM((5, count, feat), b16),
            pltpu.VMEM((feat, half), b16),
            pltpu.VMEM((feat, half), b16),
            pltpu.VMEM((half, feat), b16),
            dma((3,)),
            dma((2, 4)), dma((4,)),
            dma((4,)), dma((4,)),
            dma((2, 4)), dma((2, 4)),
            dma((2, 4)), dma((2, 4)),
            dma((4,)), dma((4,)),
            dma((4,)), dma((5,)),
        ],
        compiler_params=pltpu.CompilerParams(
            collective_id=0, has_side_effects=True, vmem_limit_bytes=48 * 2**20
        ),
    )(tokens, table, w_gate, w_up, w_down)


def solution(mesh):
    two_of_two = mesh.shape["cluster"] == 4 and mesh.shape["expert"] == 4
    shards = fused if two_of_two else routed
    in_specs = (
        P(("groups", "cluster", "expert"), None),
        P(("groups", "cluster", "expert")),
        P(("groups", "cluster", "expert"), None),
        P(("groups", "cluster", "expert"), None),
        P(("cluster", "expert"), None, None),
        P(("cluster", "expert"), None, None),
        P(("cluster", "expert"), None, None),
    )
    out_specs = P(("groups", "cluster", "expert"), None)
    return jax.shard_map(shards, mesh=mesh, in_specs=in_specs, out_specs=out_specs, check_vma=False)
```

```python
import jax
import jax.numpy as jnp
from jax import lax
from jax.experimental import pallas as pl
from jax.experimental.pallas import tpu as pltpu
from jax.sharding import PartitionSpec as P


def routed(tokens, cluster_ids, expert_ids, gate_probs, w_gate, w_up, w_down):
    clusters = lax.axis_size("cluster")
    expert_devs = lax.axis_size("expert")
    per_cluster = expert_devs // 2
    tok_count, feat_dim = tokens.shape
    cap_first = 2 * tok_count // clusters
    cap_second = 2 * cap_first // per_cluster
    stride = clusters * cap_second
    own_cluster = lax.axis_index("cluster")
    pair_key = (cluster_ids[:, None] * per_cluster + expert_ids).reshape(-1)
    pair_pos = jnp.arange(2 * tok_count)
    pair_earlier = (pair_key[:, None] == pair_key[None, :]) & (
        pair_pos[None, :] < pair_pos[:, None]
    )
    pair_slot = jnp.sum(pair_earlier.astype(jnp.int32), axis=1).reshape(tok_count, 2)
    tok_pos = jnp.arange(tok_count)
    tok_earlier = (cluster_ids[:, None] == cluster_ids[None, :]) & (
        tok_pos[None, :] < tok_pos[:, None]
    )
    tok_rank = jnp.sum(tok_earlier.astype(jnp.int32), axis=1)
    first_slot = cluster_ids * cap_first + tok_rank
    target = expert_ids * stride + own_cluster * cap_second + pair_slot
    out_rows = jnp.zeros((clusters * cap_first, feat_dim), jnp.bfloat16).at[first_slot].set(tokens)
    out_target = (
        jnp.full((clusters * cap_first, 2), per_cluster * stride, jnp.int32)
        .at[first_slot]
        .set(target)
    )
    out_gates = jnp.zeros((clusters * cap_first, 2), jnp.bfloat16).at[first_slot].set(gate_probs)
    rows_in, target_in, gates_in = (
        lax.all_to_all(
            out_rows.reshape(clusters, cap_first, feat_dim),
            "cluster",
            split_axis=0,
            concat_axis=0,
            tiled=True,
        ),
        lax.all_to_all(
            out_target.reshape(clusters, cap_first, 2),
            "cluster",
            split_axis=0,
            concat_axis=0,
            tiled=True,
        ),
        lax.all_to_all(
            out_gates.reshape(clusters, cap_first, 2),
            "cluster",
            split_axis=0,
            concat_axis=0,
            tiled=True,
        ),
    )
    flat_rows = rows_in.reshape(-1, feat_dim)
    flat_target = target_in.reshape(-1, 2)
    flat_gates = gates_in.reshape(-1, 2).astype(jnp.float32)
    sectioned = jnp.zeros((per_cluster * stride, feat_dim), jnp.bfloat16)
    sectioned = sectioned.at[flat_target[:, 0]].set(flat_rows, mode="drop")
    sectioned = sectioned.at[flat_target[:, 1]].set(flat_rows, mode="drop")
    sectioned = sectioned.reshape(per_cluster, clusters, cap_second, feat_dim)
    gate_half = w_gate[0]
    up_half = w_up[0]
    down_half = w_down[0]
    send = jnp.repeat(sectioned, 2, axis=0)
    block = lax.all_to_all(send, "expert", split_axis=0, concat_axis=2, tiled=True)
    items = block.shape[1]
    rows = block.reshape(-1, feat_dim)
    gate = jnp.dot(rows, gate_half, preferred_element_type=jnp.float32)
    up_part = jnp.dot(rows, up_half, preferred_element_type=jnp.float32)
    hidden = (jax.nn.silu(gate) * up_part).astype(jnp.bfloat16)
    partial_value = jnp.dot(hidden, down_half, preferred_element_type=jnp.float32).reshape(
        1, items, expert_devs * cap_second, feat_dim
    )
    back = lax.all_to_all(partial_value, "expert", split_axis=2, concat_axis=0, tiled=True)
    summed = jnp.sum(back.reshape(per_cluster, 2, items, cap_second, feat_dim), axis=1)
    expert_out = summed.astype(jnp.bfloat16)
    flat_out = expert_out.reshape(-1, feat_dim)
    safe_target = jnp.minimum(flat_target, per_cluster * stride - 1)
    picked = flat_out[safe_target]
    combined = (
        picked[:, 0].astype(jnp.float32) * flat_gates[:, 0:1]
        + picked[:, 1].astype(jnp.float32) * flat_gates[:, 1:2]
    )
    combined = combined.astype(jnp.bfloat16).reshape(clusters, cap_first, feat_dim)
    back_rows = lax.all_to_all(combined, "cluster", split_axis=0, concat_axis=0, tiled=True)
    return back_rows.reshape(-1, feat_dim)[first_slot]


MESH = pl.DeviceIdType.MESH
LANES = 128


def layer_kernel(
    tok_ref, cid_ref, eid_ref, prob_ref, wg_hbm, wu_hbm, wd_hbm, out_ref,
    rows, part, core_in, x_in, z_in, wg, wu, wd,
    w_sem, zs, zr, xs, xr, ss, sr, ps, pr, bs, br, cs, cr,
):
    group = lax.axis_index("groups")
    c = lax.axis_index("cluster")
    z = lax.axis_index("expert")
    count, feat = tok_ref.shape
    depth = 4
    twin = (group, c + 1 - 2 * (c % 2), z)
    across = (group, (c + 2) % 4, z)
    below, above = (group, c, z - 1), (group, c, z + 1)
    own_expert = c * 2 + z // 2

    loads = [
        pltpu.make_async_copy(src.at[0], dst, w_sem.at[i])
        for i, (src, dst) in enumerate(((wg_hbm, wg), (wu_hbm, wu), (wd_hbm, wd)))
    ]
    for load in loads:
        load.start()

    barrier = pltpu.get_barrier_semaphore()
    pl.semaphore_signal(barrier, inc=1, device_id=twin, device_id_type=MESH)
    pl.semaphore_signal(barrier, inc=1, device_id=across, device_id_type=MESH)

    @pl.when(z > 0)
    def _():
        pl.semaphore_signal(barrier, inc=1, device_id=below, device_id_type=MESH)

    @pl.when(z < depth - 1)
    def _():
        pl.semaphore_signal(barrier, inc=1, device_id=above, device_id_type=MESH)

    middle = (z > 0) & (z < depth - 1)
    rows[z, pl.ds(0, count), pl.ds(0, feat)] = tok_ref[...]
    pair = cid_ref[...] * 2 + eid_ref[...]
    probs = prob_ref[...].astype(jnp.float32)
    expert = lax.broadcasted_iota(jnp.int32, (LANES, count), 0)
    table = jnp.where(expert == pair[0:1], probs[0:1], 0.0)
    table = jnp.where(expert == pair[1:2], probs[1:2], table)
    rows[z, pl.ds(0, count), pl.ds(feat, LANES)] = table.T.astype(jnp.bfloat16)
    pl.semaphore_wait(barrier, 3 + middle.astype(jnp.int32))

    def remote(src, dst, send, recv, device):
        return pltpu.make_async_remote_copy(
            src_ref=src, dst_ref=dst, send_sem=send, recv_sem=recv,
            device_id=device, device_id_type=MESH,
        )

    part_rows = count // 2

    def block(b, r, h):
        return rows.at[b, pl.ds(r * count + h * part_rows, part_rows)]

    def whole(b, r):
        return part.at[b, pl.ds(r * count, count)]

    def piece(b, r, h):
        return part.at[b, pl.ds(r * count + h * part_rows, part_rows)]

    def cut(h):
        return pl.ds(h * part_rows, part_rows)

    def to_z(b, h, up):
        near = block(b, 0, h)
        return remote(near, near, zs.at[up, b, h], zr.at[b, h], above if up else below)

    def to_x(b, h):
        return remote(block(b, 0, h), block(b, 2, h), xs.at[b, h], xr.at[b, h], across)

    def to_twin(b, r, h):
        i = r // 2
        return remote(block(b, r, h), block(b, r + 1, h), ss.at[i, b, h], sr.at[i, b, h], twin)

    def part_to_twin(b, r):
        i = r // 2
        return remote(whole(b, r), core_in.at[i, b], ps.at[i, b], pr.at[i, b], twin)

    def part_to_x(b, h):
        return remote(piece(b, 2, h), x_in.at[b, cut(h)], bs.at[b, h], br.at[b, h], across)

    def sum_up(b, h):
        return remote(piece(b, 0, h), z_in.at[b, cut(h)], cs.at[b, h], cr.at[b, h], above)

    def sum_down(b, h):
        last = (b == z - 1).astype(jnp.int32)
        slot = b * (1 - last) + depth * last
        return remote(piece(b, 0, h), z_in.at[slot, cut(h)], cs.at[b, h], cr.at[slot, h], below)

    def order(k):
        far = 3 * (2 - z)
        inner = jnp.where(k == 0, z, jnp.where(k == 1, z - 1, jnp.where(k == 2, z + 1, far)))
        return jnp.where(z == 0, k, jnp.where(z == depth - 1, depth - 1 - k, inner))

    def spread(b, h):
        to_x(b, h).start()
        to_twin(b, 0, h).start()

    for h in (0, 1):

        @pl.when(z < depth - 1)
        def _():
            to_z(z, h, 1).start()

        @pl.when(z > 0)
        def _():
            to_z(z, h, 0).start()

        spread(z, h)

    def fold_core(b, h):
        piece(b, 2, h)[...] = piece(b, 2, h)[...] + core_in[1, b, cut(h)]
        part_to_x(b, h).start()

    def compute(b):
        lhs = rows[b, :, pl.ds(0, feat)]
        gate = jnp.dot(lhs, wg[...], preferred_element_type=jnp.float32)
        up_part = jnp.dot(lhs, wu[...], preferred_element_type=jnp.float32)
        hidden = (gate / (1.0 + jnp.exp(-gate)) * up_part).astype(jnp.bfloat16)
        weights = rows[b, :, pl.ds(feat, LANES)].astype(jnp.float32)
        lane = lax.broadcasted_iota(jnp.int32, weights.shape, 1)
        weight = jnp.sum(jnp.where(lane == own_expert, weights, 0.0), axis=1, keepdims=True)
        tile = min(feat, 512)
        for n in range(feat // tile):
            cols = pl.ds(n * tile, tile)
            out = jnp.dot(hidden, wd[:, cols], preferred_element_type=jnp.float32)
            part[b, :, cols] = (out * weight).astype(jnp.bfloat16)

    def stage(d, carry):
        for h in (0, 1):
            for side in (-1, 1):
                b = z + side * d

                @pl.when((d < depth) & (b >= 0) & (b < depth))
                def _():
                    to_z(b, h, 0).wait_recv()

                    @pl.when((z < depth - 1) if side < 0 else (z > 0))
                    def _():
                        to_z(b, h, 1 if side < 0 else 0).start()

                    spread(b, h)

        b = order(d - 1)
        for h in (0, 1):
            to_x(b, h).wait_recv()
            to_twin(b, 2, h).start()

        @pl.when(d == depth)
        def _():
            part_to_twin(z, 3).wait_recv()
            fold_core(z, 0)

        @pl.when(d == 1)
        def _():
            for load in loads:
                load.wait()

        for h in (0, 1):
            to_twin(b, 0, h).wait_recv()
            to_twin(b, 2, h).wait_recv()
        compute(b)
        part_to_twin(b, 3).start()
        part_to_twin(b, 1).start()
        return carry

    lax.fori_loop(1, depth + 1, stage, 0)
    for k in (3, 2, 1):
        part_to_twin(order(k), 3).wait_recv()
        for h in (0, 1):
            fold_core(order(k), h)
    fold_core(z, 1)

    def total(b, h):
        part_to_x(b, h).wait_recv()
        value = piece(b, 0, h)[...].astype(jnp.float32)
        value = value + core_in[0, b, cut(h)].astype(jnp.float32)
        return value + x_in[b, cut(h)].astype(jnp.float32)

    def fold(j, carry):
        b = order(depth - 1 - j)
        part_to_twin(b, 1).wait_recv()
        for h in (0, 1):
            piece(b, 0, h)[...] = total(b, h).astype(jnp.bfloat16)

            @pl.when(((b > z) & (z > 0)) | ((b < z) & (z < depth - 1)))
            def _():
                sum_up(b, h).wait_recv()
                mine = piece(b, 0, h)[...].astype(jnp.float32)
                mine = mine + z_in[b, cut(h)].astype(jnp.float32)
                piece(b, 0, h)[...] = mine.astype(jnp.bfloat16)

            @pl.when(b > z)
            def _():
                sum_up(b, h).start()

            @pl.when(b < z)
            def _():
                sum_down(b, h).start()

        return carry

    lax.fori_loop(0, depth - 1, fold, 0)
    part_to_twin(z, 1).wait_recv()
    for h in (0, 1):
        out_ref[cut(h), :] = total(z, h).astype(jnp.bfloat16)
        for slot, there in ((z, z > 0), (depth, z < depth - 1)):

            @pl.when(there)
            def _():
                inbox = z_in.at[slot, cut(h)]
                remote(piece(z, 0, h), inbox, cs.at[z, h], cr.at[slot, h], across).wait_recv()
                mine = out_ref[cut(h), :].astype(jnp.float32)
                mine = mine + z_in[slot, cut(h)].astype(jnp.float32)
                out_ref[cut(h), :] = mine.astype(jnp.bfloat16)

    def drain(b, carry):
        for h in (0, 1):

            @pl.when((z < depth - 1) & (b <= z))
            def _():
                to_z(b, h, 1).wait_send()

            @pl.when((z > 0) & (b >= z))
            def _():
                to_z(b, h, 0).wait_send()

            to_x(b, h).wait_send()
            to_twin(b, 0, h).wait_send()
            to_twin(b, 2, h).wait_send()
            part_to_x(b, h).wait_send()

            @pl.when(b != z)
            def _():
                sum_up(b, h).wait_send()

        part_to_twin(b, 1).wait_send()
        part_to_twin(b, 3).wait_send()
        return carry

    lax.fori_loop(0, depth, drain, 0)


def fused(tokens, cluster_ids, expert_ids, gate_probs, w_gate, w_up, w_down):
    count, feat = tokens.shape
    half = w_gate.shape[2]
    vmem = pl.BlockSpec(memory_space=pltpu.VMEM)
    hbm = pl.BlockSpec(memory_space=pl.ANY)
    b16 = jnp.bfloat16
    dma = pltpu.SemaphoreType.DMA
    return pl.pallas_call(
        layer_kernel,
        out_shape=jax.ShapeDtypeStruct((count, feat), b16),
        in_specs=[vmem, vmem, vmem, vmem, hbm, hbm, hbm],
        out_specs=vmem,
        scratch_shapes=[
            pltpu.VMEM((4, 4 * count, feat + LANES), b16),
            pltpu.VMEM((4, 4 * count, feat), b16),
            pltpu.VMEM((2, 4, count, feat), b16),
            pltpu.VMEM((4, count, feat), b16),
            pltpu.VMEM((5, count, feat), b16),
            pltpu.VMEM((feat, half), b16),
            pltpu.VMEM((feat, half), b16),
            pltpu.VMEM((half, feat), b16),
            dma((3,)),
            dma((2, 4, 2)), dma((4, 2)),
            dma((4, 2)), dma((4, 2)),
            dma((2, 4, 2)), dma((2, 4, 2)),
            dma((2, 4)), dma((2, 4)),
            dma((4, 2)), dma((4, 2)),
            dma((4, 2)), dma((5, 2)),
        ],
        compiler_params=pltpu.CompilerParams(
            collective_id=0, has_side_effects=True, vmem_limit_bytes=62 * 2**20
        ),
    )(tokens, cluster_ids[None, :], expert_ids.T, gate_probs.T, w_gate, w_up, w_down)


def solution(mesh):
    two_of_two = mesh.shape["cluster"] == 4 and mesh.shape["expert"] == 4
    shards = fused if two_of_two else routed
    in_specs = (
        P(("groups", "cluster", "expert"), None),
        P(("groups", "cluster", "expert")),
        P(("groups", "cluster", "expert"), None),
        P(("groups", "cluster", "expert"), None),
        P(("cluster", "expert"), None, None),
        P(("cluster", "expert"), None, None),
        P(("cluster", "expert"), None, None),
    )
    out_specs = P(("groups", "cluster", "expert"), None)
    return jax.shard_map(shards, mesh=mesh, in_specs=in_specs, out_specs=out_specs, check_vma=False)
```

```python
import jax
import jax.numpy as jnp
from jax import lax
from jax.experimental import pallas as pl
from jax.experimental.pallas import tpu as pltpu
from jax.sharding import PartitionSpec as P


def routed(tokens, cluster_ids, expert_ids, gate_probs, w_gate, w_up, w_down):
    clusters = lax.axis_size("cluster")
    expert_devs = lax.axis_size("expert")
    per_cluster = expert_devs // 2
    tok_count, feat_dim = tokens.shape
    cap_first = 2 * tok_count // clusters
    cap_second = 2 * cap_first // per_cluster
    stride = clusters * cap_second
    own_cluster = lax.axis_index("cluster")
    pair_key = (cluster_ids[:, None] * per_cluster + expert_ids).reshape(-1)
    pair_pos = jnp.arange(2 * tok_count)
    pair_earlier = (pair_key[:, None] == pair_key[None, :]) & (
        pair_pos[None, :] < pair_pos[:, None]
    )
    pair_slot = jnp.sum(pair_earlier.astype(jnp.int32), axis=1).reshape(tok_count, 2)
    tok_pos = jnp.arange(tok_count)
    tok_earlier = (cluster_ids[:, None] == cluster_ids[None, :]) & (
        tok_pos[None, :] < tok_pos[:, None]
    )
    tok_rank = jnp.sum(tok_earlier.astype(jnp.int32), axis=1)
    first_slot = cluster_ids * cap_first + tok_rank
    target = expert_ids * stride + own_cluster * cap_second + pair_slot
    out_rows = jnp.zeros((clusters * cap_first, feat_dim), jnp.bfloat16).at[first_slot].set(tokens)
    out_target = (
        jnp.full((clusters * cap_first, 2), per_cluster * stride, jnp.int32)
        .at[first_slot]
        .set(target)
    )
    out_gates = jnp.zeros((clusters * cap_first, 2), jnp.bfloat16).at[first_slot].set(gate_probs)
    rows_in, target_in, gates_in = (
        lax.all_to_all(
            out_rows.reshape(clusters, cap_first, feat_dim),
            "cluster",
            split_axis=0,
            concat_axis=0,
            tiled=True,
        ),
        lax.all_to_all(
            out_target.reshape(clusters, cap_first, 2),
            "cluster",
            split_axis=0,
            concat_axis=0,
            tiled=True,
        ),
        lax.all_to_all(
            out_gates.reshape(clusters, cap_first, 2),
            "cluster",
            split_axis=0,
            concat_axis=0,
            tiled=True,
        ),
    )
    flat_rows = rows_in.reshape(-1, feat_dim)
    flat_target = target_in.reshape(-1, 2)
    flat_gates = gates_in.reshape(-1, 2).astype(jnp.float32)
    sectioned = jnp.zeros((per_cluster * stride, feat_dim), jnp.bfloat16)
    sectioned = sectioned.at[flat_target[:, 0]].set(flat_rows, mode="drop")
    sectioned = sectioned.at[flat_target[:, 1]].set(flat_rows, mode="drop")
    sectioned = sectioned.reshape(per_cluster, clusters, cap_second, feat_dim)
    gate_half = w_gate[0]
    up_half = w_up[0]
    down_half = w_down[0]
    send = jnp.repeat(sectioned, 2, axis=0)
    block = lax.all_to_all(send, "expert", split_axis=0, concat_axis=2, tiled=True)
    items = block.shape[1]
    rows = block.reshape(-1, feat_dim)
    gate = jnp.dot(rows, gate_half, preferred_element_type=jnp.float32)
    up_part = jnp.dot(rows, up_half, preferred_element_type=jnp.float32)
    hidden = (jax.nn.silu(gate) * up_part).astype(jnp.bfloat16)
    partial_value = jnp.dot(hidden, down_half, preferred_element_type=jnp.float32).reshape(
        1, items, expert_devs * cap_second, feat_dim
    )
    back = lax.all_to_all(partial_value, "expert", split_axis=2, concat_axis=0, tiled=True)
    summed = jnp.sum(back.reshape(per_cluster, 2, items, cap_second, feat_dim), axis=1)
    expert_out = summed.astype(jnp.bfloat16)
    flat_out = expert_out.reshape(-1, feat_dim)
    safe_target = jnp.minimum(flat_target, per_cluster * stride - 1)
    picked = flat_out[safe_target]
    combined = (
        picked[:, 0].astype(jnp.float32) * flat_gates[:, 0:1]
        + picked[:, 1].astype(jnp.float32) * flat_gates[:, 1:2]
    )
    combined = combined.astype(jnp.bfloat16).reshape(clusters, cap_first, feat_dim)
    back_rows = lax.all_to_all(combined, "cluster", split_axis=0, concat_axis=0, tiled=True)
    return back_rows.reshape(-1, feat_dim)[first_slot]


MESH = pl.DeviceIdType.MESH
LANES = 128


def layer_kernel(
    tok_ref, cid_ref, eid_ref, prob_ref, wg_hbm, wu_hbm, wd_hbm, out_ref,
    rows, part, core_in, x_in, z_in, wg, wu, wd,
    w_sem, zs, zr, xs, xr, ss, sr, ps, pr, bs, br, cs, cr,
):
    group = lax.axis_index("groups")
    c = lax.axis_index("cluster")
    z = lax.axis_index("expert")
    count, feat = tok_ref.shape
    depth = 4
    twin = (group, c + 1 - 2 * (c % 2), z)
    across = (group, (c + 2) % 4, z)
    below, above = (group, c, z - 1), (group, c, z + 1)
    own_expert = c * 2 + z // 2

    loads = [
        pltpu.make_async_copy(src.at[0], dst, w_sem.at[i])
        for i, (src, dst) in enumerate(((wg_hbm, wg), (wu_hbm, wu), (wd_hbm, wd)))
    ]
    for load in loads:
        load.start()

    barrier = pltpu.get_barrier_semaphore()
    pl.semaphore_signal(barrier, inc=1, device_id=twin, device_id_type=MESH)
    pl.semaphore_signal(barrier, inc=1, device_id=across, device_id_type=MESH)

    @pl.when(z > 0)
    def _():
        pl.semaphore_signal(barrier, inc=1, device_id=below, device_id_type=MESH)

    @pl.when(z < depth - 1)
    def _():
        pl.semaphore_signal(barrier, inc=1, device_id=above, device_id_type=MESH)

    middle = (z > 0) & (z < depth - 1)
    rows[z, pl.ds(0, count), pl.ds(0, feat)] = tok_ref[...]
    pair = cid_ref[...] * 2 + eid_ref[...]
    probs = prob_ref[...].astype(jnp.float32)
    expert = lax.broadcasted_iota(jnp.int32, (LANES, count), 0)
    table = jnp.where(expert == pair[0:1], probs[0:1], 0.0)
    table = jnp.where(expert == pair[1:2], probs[1:2], table)
    rows[z, pl.ds(0, count), pl.ds(feat, LANES)] = table.T.astype(jnp.bfloat16)
    pl.semaphore_wait(barrier, 3 + middle.astype(jnp.int32))

    def remote(src, dst, send, recv, device):
        return pltpu.make_async_remote_copy(
            src_ref=src, dst_ref=dst, send_sem=send, recv_sem=recv,
            device_id=device, device_id_type=MESH,
        )

    part_rows = count // 2

    def block(b, r, h):
        return rows.at[b, pl.ds(r * count + h * part_rows, part_rows)]

    def whole(b, r):
        return part.at[b, pl.ds(r * count, count)]

    def piece(b, r, h):
        return part.at[b, pl.ds(r * count + h * part_rows, part_rows)]

    def cut(h):
        return pl.ds(h * part_rows, part_rows)

    def to_z(b, h, up):
        near = block(b, 0, h)
        return remote(near, near, zs.at[up, b, h], zr.at[b, h], above if up else below)

    def to_x(b, h):
        return remote(block(b, 0, h), block(b, 2, h), xs.at[b, h], xr.at[b, h], across)

    def to_twin(b, r, h):
        i = r // 2
        return remote(block(b, r, h), block(b, r + 1, h), ss.at[i, b, h], sr.at[i, b, h], twin)

    def part_to_twin(b, r):
        i = r // 2
        return remote(whole(b, r), core_in.at[i, b], ps.at[i, b], pr.at[i, b], twin)

    def part_to_x(b, h):
        return remote(piece(b, 2, h), x_in.at[b, cut(h)], bs.at[b, h], br.at[b, h], across)

    def sum_up(b, h):
        return remote(piece(b, 0, h), z_in.at[b, cut(h)], cs.at[b, h], cr.at[b, h], above)

    def sum_down(b, h):
        last = (b == z - 1).astype(jnp.int32)
        slot = b * (1 - last) + depth * last
        return remote(piece(b, 0, h), z_in.at[slot, cut(h)], cs.at[b, h], cr.at[slot, h], below)

    def order(k):
        far = 3 * (2 - z)
        inner = jnp.where(k == 0, z, jnp.where(k == 1, z - 1, jnp.where(k == 2, z + 1, far)))
        return jnp.where(z == 0, k, jnp.where(z == depth - 1, depth - 1 - k, inner))

    def spread(b, h):
        to_x(b, h).start()
        to_twin(b, 0, h).start()

    for h in (0, 1):

        @pl.when(z < depth - 1)
        def _():
            to_z(z, h, 1).start()

        @pl.when(z > 0)
        def _():
            to_z(z, h, 0).start()

        spread(z, h)

    def fold_core(b, h):
        piece(b, 2, h)[...] = piece(b, 2, h)[...] + core_in[1, b, cut(h)]
        part_to_x(b, h).start()

    def compute(b, half):
        span = pl.ds(half * 2 * count, 2 * count)
        lhs = rows[b, span, pl.ds(0, feat)]
        gate = jnp.dot(lhs, wg[...], preferred_element_type=jnp.float32)
        up_part = jnp.dot(lhs, wu[...], preferred_element_type=jnp.float32)
        hidden = (gate / (1.0 + jnp.exp(-gate)) * up_part).astype(jnp.bfloat16)
        weights = rows[b, span, pl.ds(feat, LANES)].astype(jnp.float32)
        lane = lax.broadcasted_iota(jnp.int32, weights.shape, 1)
        weight = jnp.sum(jnp.where(lane == own_expert, weights, 0.0), axis=1, keepdims=True)
        tile = min(feat, 512)
        for n in range(feat // tile):
            cols = pl.ds(n * tile, tile)
            out = jnp.dot(hidden, wd[:, cols], preferred_element_type=jnp.float32)
            part[b, span, cols] = (out * weight).astype(jnp.bfloat16)

    def stage(d, carry):
        for h in (0, 1):
            for side in (-1, 1):
                b = z + side * d

                @pl.when((d < depth) & (b >= 0) & (b < depth))
                def _():
                    to_z(b, h, 0).wait_recv()

                    @pl.when((z < depth - 1) if side < 0 else (z > 0))
                    def _():
                        to_z(b, h, 1 if side < 0 else 0).start()

                    spread(b, h)

        b = order(d - 1)

        @pl.when(d == 1)
        def _():
            for load in loads:
                load.wait()

        for h in (0, 1):
            to_twin(b, 0, h).wait_recv()
        compute(b, 0)
        part_to_twin(b, 1).start()
        for h in (0, 1):
            to_x(b, h).wait_recv()
            to_twin(b, 2, h).start()

        @pl.when(d == depth)
        def _():
            part_to_twin(z, 3).wait_recv()
            fold_core(z, 0)

        for h in (0, 1):
            to_twin(b, 2, h).wait_recv()
        compute(b, 1)
        part_to_twin(b, 3).start()
        return carry

    lax.fori_loop(1, depth + 1, stage, 0)
    for k in (3, 2, 1):
        part_to_twin(order(k), 3).wait_recv()
        for h in (0, 1):
            fold_core(order(k), h)
    fold_core(z, 1)

    def total(b, h):
        part_to_x(b, h).wait_recv()
        value = piece(b, 0, h)[...].astype(jnp.float32)
        value = value + core_in[0, b, cut(h)].astype(jnp.float32)
        return value + x_in[b, cut(h)].astype(jnp.float32)

    def fold(j, carry):
        b = order(depth - 1 - j)
        part_to_twin(b, 1).wait_recv()
        for h in (0, 1):
            piece(b, 0, h)[...] = total(b, h).astype(jnp.bfloat16)

            @pl.when(((b > z) & (z > 0)) | ((b < z) & (z < depth - 1)))
            def _():
                sum_up(b, h).wait_recv()
                mine = piece(b, 0, h)[...].astype(jnp.float32)
                mine = mine + z_in[b, cut(h)].astype(jnp.float32)
                piece(b, 0, h)[...] = mine.astype(jnp.bfloat16)

            @pl.when(b > z)
            def _():
                sum_up(b, h).start()

            @pl.when(b < z)
            def _():
                sum_down(b, h).start()

        return carry

    lax.fori_loop(0, depth - 1, fold, 0)
    part_to_twin(z, 1).wait_recv()
    for h in (0, 1):
        out_ref[cut(h), :] = total(z, h).astype(jnp.bfloat16)
        for slot, there in ((z, z > 0), (depth, z < depth - 1)):

            @pl.when(there)
            def _():
                inbox = z_in.at[slot, cut(h)]
                remote(piece(z, 0, h), inbox, cs.at[z, h], cr.at[slot, h], across).wait_recv()
                mine = out_ref[cut(h), :].astype(jnp.float32)
                mine = mine + z_in[slot, cut(h)].astype(jnp.float32)
                out_ref[cut(h), :] = mine.astype(jnp.bfloat16)

    def drain(b, carry):
        for h in (0, 1):

            @pl.when((z < depth - 1) & (b <= z))
            def _():
                to_z(b, h, 1).wait_send()

            @pl.when((z > 0) & (b >= z))
            def _():
                to_z(b, h, 0).wait_send()

            to_x(b, h).wait_send()
            to_twin(b, 0, h).wait_send()
            to_twin(b, 2, h).wait_send()
            part_to_x(b, h).wait_send()

            @pl.when(b != z)
            def _():
                sum_up(b, h).wait_send()

        part_to_twin(b, 1).wait_send()
        part_to_twin(b, 3).wait_send()
        return carry

    lax.fori_loop(0, depth, drain, 0)


def fused(tokens, cluster_ids, expert_ids, gate_probs, w_gate, w_up, w_down):
    count, feat = tokens.shape
    half = w_gate.shape[2]
    vmem = pl.BlockSpec(memory_space=pltpu.VMEM)
    hbm = pl.BlockSpec(memory_space=pl.ANY)
    b16 = jnp.bfloat16
    dma = pltpu.SemaphoreType.DMA
    return pl.pallas_call(
        layer_kernel,
        out_shape=jax.ShapeDtypeStruct((count, feat), b16),
        in_specs=[vmem, vmem, vmem, vmem, hbm, hbm, hbm],
        out_specs=vmem,
        scratch_shapes=[
            pltpu.VMEM((4, 4 * count, feat + LANES), b16),
            pltpu.VMEM((4, 4 * count, feat), b16),
            pltpu.VMEM((2, 4, count, feat), b16),
            pltpu.VMEM((4, count, feat), b16),
            pltpu.VMEM((5, count, feat), b16),
            pltpu.VMEM((feat, half), b16),
            pltpu.VMEM((feat, half), b16),
            pltpu.VMEM((half, feat), b16),
            dma((3,)),
            dma((2, 4, 2)), dma((4, 2)),
            dma((4, 2)), dma((4, 2)),
            dma((2, 4, 2)), dma((2, 4, 2)),
            dma((2, 4)), dma((2, 4)),
            dma((4, 2)), dma((4, 2)),
            dma((4, 2)), dma((5, 2)),
        ],
        compiler_params=pltpu.CompilerParams(
            collective_id=0, has_side_effects=True, vmem_limit_bytes=62 * 2**20
        ),
    )(tokens, cluster_ids[None, :], expert_ids.T, gate_probs.T, w_gate, w_up, w_down)


def solution(mesh):
    two_of_two = mesh.shape["cluster"] == 4 and mesh.shape["expert"] == 4
    shards = fused if two_of_two else routed
    in_specs = (
        P(("groups", "cluster", "expert"), None),
        P(("groups", "cluster", "expert")),
        P(("groups", "cluster", "expert"), None),
        P(("groups", "cluster", "expert"), None),
        P(("cluster", "expert"), None, None),
        P(("cluster", "expert"), None, None),
        P(("cluster", "expert"), None, None),
    )
    out_specs = P(("groups", "cluster", "expert"), None)
    return jax.shard_map(shards, mesh=mesh, in_specs=in_specs, out_specs=out_specs, check_vma=False)
```
